256 devices in a mesh: pipe: 16 (over z, x_lo), expert: 16 (over y, x_hi, core).
Axes of the slice: x: 4 (x_hi: 2, x_lo: 2; x = x_hi * 2 + x_lo), y: 4, z: 8, core: 2. Of those that a mesh axis runs over, the one named last changes fastest.
Arguments:
- flight: bfloat16 [16, 2048, 4096], P('pipe', 'expert'), may hold values from -6 to 6
- norm_gain: float32 [16, 4096], P('pipe'), may hold values from 0.5 to 2
- router: bfloat16 [16, 4096, 8], P('pipe'), may hold values from -0.09375 to 0.09375
- w_gate: bfloat16 [16, 4096, 6144], P('pipe', None, 'expert'), may hold values from -0.09375 to 0.09375
- w_up: bfloat16 [16, 4096, 6144], P('pipe', None, 'expert'), may hold values from -0.09375 to 0.09375
- w_down: bfloat16 [16, 6144, 4096], P('pipe', 'expert'), may hold values from -0.21875 to 0.21875
- routes: int32 [16, 2, 2048, 2], P('pipe', None, 'expert'), may hold values from 0 to 7, all different within a row; in each aligned block of 128 rows (0 to 127, 128 to 255, ..., all dimensions but the last counted through in order) at most 48 rows name the same one
Outputs:
- landed: bfloat16 [16, 2048, 4096], P('pipe', 'expert')
The draws below stay inside these ranges and needn't reach their ends.
Inputs may be any that keep to these rules, and one draw needn't show every extreme that they name: `routes`: each row names 2 different experts. In each aligned block of 128 rows (the rows of one device for one section and step) no expert is named by more than 48 rows, and in some block an expert is named by exactly 48 rows.
All inputs are finite; a program needn't handle non-finite values.
Results may differ from the reference program's by a relative error of at most 0.0084.
Values may be sent and summed in bfloat16 or wider, within the bound.
No kernel may reach another device: no remote copies, remote signals or barrier semaphores. Data moves between devices by JAX's collectives and lax.ppermute only.
A program may use at most 128 MiB of HBM per device.

```python
import math
import jax
import jax.numpy as jnp
import numpy as np
from jax import lax

D = 4096
HID = 768
TOPK = 2
TICKS = 2
R = 128
SECTIONS = 16
EXPERTS = 8
TOKENS = 2048
CAP = 48
N_EXPERT = 16


def levels(key, shape, split, least, high):
    def one(dim, blocks):
        steps = jax.random.uniform(jax.random.fold_in(jax.random.fold_in(key, 6), dim), (blocks,), jnp.float32, least / len(split), high / len(split))
        return jnp.repeat(jnp.exp(steps), shape[dim] // blocks).reshape((-1,) + (1,) * (len(shape) - dim - 1))

    gain = one(*split[0])
    for cut in split[1:]:
        gain = gain * one(*cut)
    return gain


def assign_block(stream_key, own, number, rows, count, top, bound, lean):
    order = jax.random.permutation(stream_key, count)
    crowded, ordinary = load_shares(count, rows * top, bound, lean, True), load_shares(count, rows * top, bound, lean, False)
    places = jnp.arange(count)

    def named(tallies, rotation):
        used = int((tallies > 0).sum())
        fixed = max(1, used // 4)
        passed = fixed + (places - fixed + rotation * (used - fixed)) % max(1, count - fixed)
        return jnp.zeros((count,), jnp.int32).at[order[jnp.where(places < fixed, places, passed)]].set(jnp.asarray(tallies, jnp.int32))

    tallies = jnp.where(number % 4 == 0, named(crowded, number // 4), named(ordinary, number - number // 4 - 1))
    mixed = jax.random.permutation(jax.random.fold_in(own, 3), count)
    giver, sink = mixed[0:count // 2 * 2:2], mixed[1:count // 2 * 2:2]
    slack = jnp.minimum(tallies[giver] - 1, bound - tallies[sink]) // 2
    slack = jnp.where((giver == order[0]) | (sink == order[0]) | (tallies[sink] == 0), 0, jnp.maximum(slack, 0))
    passed = jax.random.randint(jax.random.fold_in(own, 4), (count // 2,), 0, 1 << 20) % (slack + 1)
    tallies = tallies.at[giver].add(-passed).at[sink].add(passed)
    labels = jnp.searchsorted(jnp.cumsum(tallies), jnp.arange(rows * top), side="right").astype(jnp.int32)
    grid = labels.reshape(top, rows).T
    grid = grid[jax.random.permutation(jax.random.fold_in(own, 1), rows)]
    rotation = jax.random.randint(jax.random.fold_in(own, 2), (rows, 1), 0, top)
    return jnp.take_along_axis(grid, (jnp.arange(top)[None, :] + rotation) % top, axis=1)


def load_shares(amount, total, bound, slope, full):
    weights = [(1 << 20) // math.isqrt(standing ** slope) + 1 for standing in range(1, amount + 1)]
    largest = bound if full else min(bound, max(-(-total // amount), total * weights[0] // sum(weights)))
    least = 1 if total - largest >= amount - 1 else 0
    given, surplus = [largest] + [least] * (amount - 1), total - largest - least * (amount - 1)
    while surplus > 0:
        candidates = [i for i in range(1, amount) if given[i] < largest] or [i for i in range(1, amount) if given[i] < bound]
        whole, budget = sum([weights[i] for i in candidates]), surplus
        for i in candidates:
            addition = min(bound - given[i], max(1, budget * weights[i] // whole), surplus)
            given[i] = given[i] + addition
            surplus = surplus - addition
    return np.array(given)


def gaussian(stream_key, shape, deviation, most, pieces=(), kind=jnp.bfloat16):
    entries = deviation * jax.random.normal(stream_key, shape, jnp.float32)
    if pieces:
        entries = entries * levels(stream_key, shape, pieces, -0.22, 0.18)
    return jnp.clip(entries, -most, most).astype(kind)


def setup_inputs(seed: int = 0) -> dict:
    streams_of = jax.random.split(jax.random.key(seed), 8)
    flight = gaussian(streams_of[0], (SECTIONS, TOKENS, D), 1.0, 6.0, ((0, 16), (1, 16)))
    norm_gain = jnp.clip(0.5 + 1.5 * jax.random.uniform(streams_of[1], (SECTIONS, D), jnp.float32) ** levels(streams_of[1], (SECTIONS, D), ((0, 16),), -0.2, 0.2), 0.5, 2.0)
    router = gaussian(streams_of[2], (SECTIONS, D, EXPERTS), D ** -0.5, 0.09375, ((0, 16),))
    w_gate = gaussian(streams_of[3], (SECTIONS, D, EXPERTS * HID), D ** -0.5, 0.09375, ((0, 16), (2, 16)))
    w_up = gaussian(streams_of[4], (SECTIONS, D, EXPERTS * HID), D ** -0.5, 0.09375, ((0, 16), (2, 16)))
    w_down = gaussian(streams_of[5], (SECTIONS, EXPERTS * HID, D), HID ** -0.5, 0.21875, ((0, 16), (1, 16)))
    routes_keys = jax.random.split(jax.random.fold_in(streams_of[6], 1), SECTIONS * TICKS * TOKENS // R)
    routes_turns = jax.random.permutation(jax.random.fold_in(streams_of[6], 3), SECTIONS * TICKS * TOKENS // R)
    routes = jax.vmap(lambda own, number: assign_block(jax.random.fold_in(streams_of[6], 2), own, number, R, EXPERTS, TOPK, CAP, 2))(routes_keys, routes_turns).reshape((SECTIONS, TICKS, TOKENS, TOPK))
    return {"flight": flight, "norm_gain": norm_gain, "router": router, "w_gate": w_gate, "w_up": w_up, "w_down": w_down, "routes": routes}


def build_slots(block, route_ids, experts, capacity):
    rows_local = block.shape[0]
    top_count = route_ids.shape[1]
    flat_ids = route_ids.reshape(-1).astype(jnp.int32)
    onehot = (flat_ids[:, None] == jnp.arange(experts, dtype=jnp.int32)[None, :]).astype(jnp.int32)
    before = jnp.cumsum(onehot, axis=0) - onehot
    position = lax.optimization_barrier(jnp.sum(before * onehot, axis=1))
    slot_index = (flat_ids * capacity + position).astype(jnp.int32)
    source_row = (jnp.arange(rows_local * top_count, dtype=jnp.int32) // top_count + 1).astype(jnp.int32)
    slot_table = jnp.zeros((experts * capacity,), jnp.int32).at[slot_index].set(source_row)
    padded = jnp.concatenate([jnp.zeros((1, block.shape[1]), block.dtype), block], axis=0)
    return (slot_index, jnp.take(padded, slot_table, axis=0))

def expert_apply(rows, gate_cols, up_cols, down_rows):
    half_units = gate_cols.shape[1] // 2
    partials = []
    for half_index in range(2):
        lower = half_index * half_units
        gate_act = jnp.dot(rows, gate_cols[:, lower:lower + half_units], preferred_element_type=jnp.float32)
        up_act = jnp.dot(rows, up_cols[:, lower:lower + half_units], preferred_element_type=jnp.float32)
        hidden = (jax.nn.silu(gate_act) * up_act).astype(jnp.bfloat16)
        partial_value = jnp.dot(hidden, down_rows[lower:lower + half_units, :], preferred_element_type=jnp.float32).astype(jnp.bfloat16)
        partial_value = lax.optimization_barrier(partial_value)
        partials.append(partial_value.astype(jnp.float32))
    return (partials[0] + partials[1]).astype(jnp.bfloat16)

def section_step(inputs):
    current, norm_gain, router, w_gate, w_up, w_down, route_ids = inputs
    model_width = current.shape[1]
    experts = router.shape[1]
    float_state = current.astype(jnp.float32)
    normed = (float_state * lax.rsqrt(lax.optimization_barrier(jnp.mean(float_state * float_state, axis=-1, keepdims=True)) + 1e-06) * norm_gain[None, :]).astype(jnp.bfloat16)
    logits = jnp.dot(normed, router, preferred_element_type=jnp.float32)
    chosen = jnp.take_along_axis(logits, route_ids, axis=1)
    raised = jnp.exp(chosen)
    mix_weight = raised / lax.optimization_barrier(jnp.sum(raised, axis=1, keepdims=True))
    blocks = normed.reshape(N_EXPERT, R, model_width)
    block_ids = route_ids.reshape(N_EXPERT, R, TOPK)
    slot_index, buffers = jax.vmap(lambda blk, bid: build_slots(blk, bid, experts, CAP))(blocks, block_ids)
    by_expert = buffers.reshape(N_EXPERT, experts, CAP, model_width).transpose(1, 0, 2, 3).reshape(experts, N_EXPERT * CAP, model_width)
    gate_split = w_gate.reshape(model_width, experts, HID).transpose(1, 0, 2)
    up_split = w_up.reshape(model_width, experts, HID).transpose(1, 0, 2)
    down_split = w_down.reshape(experts, HID, model_width)
    outputs = lax.map(lambda item: expert_apply(item[0], item[1], item[2], item[3]), (by_expert, gate_split, up_split, down_split))
    outputs = outputs.reshape(experts, N_EXPERT, CAP, model_width).transpose(1, 0, 2, 3).reshape(N_EXPERT, experts * CAP, model_width)
    gathered = jax.vmap(lambda out_blk, slots: jnp.take(out_blk, slots, axis=0))(outputs, slot_index)
    gathered = gathered.reshape(N_EXPERT * R, TOPK, model_width)
    moe = lax.optimization_barrier(jnp.sum(mix_weight[:, :, None] * gathered.astype(jnp.float32), axis=1))
    return (float_state + moe).astype(jnp.bfloat16)

def reference(flight, norm_gain, router, w_gate, w_up, w_down, routes):
    current = flight
    for step_index in range(TICKS):
        current = lax.map(section_step, (current, norm_gain, router, w_gate, w_up, w_down, routes[:, step_index]))
        current = jnp.roll(current, 1, axis=0)
    return current
```

```python
import jax
import jax.numpy as jnp
from jax import lax
from jax.sharding import PartitionSpec as P


def passed_along(value, axis, steps):
    count = lax.axis_size(axis)
    pairs = [(source, (source + steps) % count) for source in range(count)]
    return lax.ppermute(value, axis, pairs)


def other_core(value):
    count = lax.axis_size("expert")
    return lax.ppermute(value, "expert", [(d, d ^ 1) for d in range(count)])


def slot_onehot(route_ids, experts, capacity):
    rows = route_ids.shape[0]
    ids = jnp.arange(experts, dtype=jnp.int32)
    named = jnp.any(route_ids[:, :, None] == ids[None, None, :], axis=1)
    earlier = jnp.arange(rows)[:, None] > jnp.arange(rows)[None, :]
    position = jnp.dot(
        earlier.astype(jnp.bfloat16), named.astype(jnp.bfloat16), preferred_element_type=jnp.float32
    )
    position = jnp.where(named, position, -1.0).T
    slots = jnp.arange(capacity, dtype=jnp.float32)
    onehot = position[:, None, :] == slots[None, :, None]
    return named, onehot.reshape(experts * capacity, rows)


def body(flight, norm_gain, router, w_gate, w_up, w_down, routes):
    rows_local = flight.shape[1]
    model_width = flight.shape[2]
    experts = router.shape[2]
    top_count = routes.shape[3]
    capacity = 2 * min(rows_local // 2, 3 * rows_local * top_count // (4 * experts))
    count = lax.axis_size("expert")
    groups = [list(range(core, count, 2)) for core in range(2)]
    gates = (w_gate[0], other_core(w_gate[0]))
    ups = (w_up[0], other_core(w_up[0]))
    downs = (w_down[0], other_core(w_down[0]))
    current = flight[0]
    for step_index in range(routes.shape[1]):
        float_state = current.astype(jnp.float32)
        normed = (
            float_state
            * lax.rsqrt(jnp.mean(float_state * float_state, axis=-1, keepdims=True) + 1e-06)
            * norm_gain[0][None, :]
        ).astype(jnp.bfloat16)
        named, onehot = slot_onehot(routes[0, step_index], experts, capacity)
        outgoing = jnp.dot(
            onehot.astype(jnp.bfloat16), normed, preferred_element_type=jnp.float32
        ).astype(jnp.bfloat16)
        arrived = lax.all_to_all(
            outgoing.reshape(experts, capacity, model_width),
            "expert",
            split_axis=0,
            concat_axis=0,
            tiled=True,
            axis_index_groups=groups,
        ).reshape(experts * capacity, model_width)
        logits = jnp.dot(normed, router[0], preferred_element_type=jnp.float32)
        raised = jnp.where(named, jnp.exp(logits), 0.0)
        mix_weight = raised / jnp.sum(raised, axis=1, keepdims=True)
        spread = jnp.where(
            onehot.reshape(experts, capacity, rows_local), mix_weight.T[:, None, :], 0.0
        ).reshape(experts * capacity, rows_local)
        spread_high = spread.astype(jnp.bfloat16)
        spread_low = (spread - spread_high.astype(jnp.float32)).astype(jnp.bfloat16)
        total = 0.0
        for gate, up, down in zip(gates, ups, downs):
            gate_act = jnp.dot(arrived, gate, preferred_element_type=jnp.float32)
            up_act = jnp.dot(arrived, up, preferred_element_type=jnp.float32)
            hidden = (jax.nn.silu(gate_act) * up_act).astype(jnp.bfloat16)
            total = total + jnp.dot(hidden, down, preferred_element_type=jnp.float32)
        returned = lax.all_to_all(
            total.astype(jnp.bfloat16).reshape(experts, capacity, model_width),
            "expert",
            split_axis=0,
            concat_axis=0,
            tiled=True,
            axis_index_groups=groups,
        ).reshape(experts * capacity, model_width)
        down_axis = (((0,), (0,)), ((), ()))
        moe = lax.dot_general(
            spread_high, returned, down_axis, preferred_element_type=jnp.float32
        ) + lax.dot_general(spread_low, returned, down_axis, preferred_element_type=jnp.float32)
        current = (float_state + moe).astype(jnp.bfloat16)
        current = passed_along(current, "pipe", 1)
    return current[None]


def solution(mesh):
    return jax.shard_map(
        body,
        mesh=mesh,
        in_specs=(
            P("pipe", "expert", None),
            P("pipe", None),
            P("pipe", None, None),
            P("pipe", None, "expert"),
            P("pipe", None, "expert"),
            P("pipe", "expert", None),
            P("pipe", None, "expert", None),
        ),
        out_specs=P("pipe", "expert", None),
        check_vma=False,
    )
```

```python
import functools

import jax
import jax.numpy as jnp
from jax import lax
from jax.experimental import pallas as pl
from jax.experimental.pallas import tpu as pltpu
from jax.sharding import PartitionSpec as P

DEEP = 1024
WIDE = 1024


def dot(a, b):
    return jnp.dot(a, b, preferred_element_type=jnp.float32)


def split_high_low(value):
    high = value.astype(jnp.bfloat16)
    return high, (value - high.astype(jnp.float32)).astype(jnp.bfloat16)


def to_core(value):
    count = lax.axis_size("expert")
    return lax.ppermute(value, "expert", [(d, d ^ 1) for d in range(count)])


def to_next(value):
    sections = lax.axis_size("pipe")
    return lax.ppermute(value, "pipe", [(p, (p + 1) % sections) for p in range(sections)])


def exchanged(value, experts):
    count = lax.axis_size("expert")
    groups = [list(range(core, count, 2)) for core in range(2)]
    slots, width = value.shape
    swapped = lax.all_to_all(
        value.reshape(experts, slots // experts, width),
        "expert",
        split_axis=0,
        concat_axis=0,
        tiled=True,
        axis_index_groups=groups,
    )
    return swapped.reshape(slots, width)


def expert_kernel(
    x_ref, g0, g1, u0, u1, d0, d1, out_ref, x, w_in, w_out, acc, hidden, outs,
    x_sem, in_sem, down_sem, out_sem,
):
    width = x.shape[1]
    half = g0.shape[1]
    units = 2 * half
    deep_count, wide_count = width // DEEP, width // WIDE

    def x_copy(k):
        cut = pl.ds(k * DEEP, DEEP)
        return pltpu.make_async_copy(x_ref.at[:, cut], x.at[:, cut], x_sem.at[k])

    def in_copy(k, j):
        source = (g0, g1, u0, u1)[j]
        cut = pl.ds(k * DEEP, DEEP)
        target = w_in.at[cut, pl.ds(j * half, half)]
        return pltpu.make_async_copy(source.at[cut, :], target, in_sem.at[k, j])

    def down_copy(n, j):
        cut = pl.ds(n * WIDE, WIDE)
        target = w_out.at[pl.ds(j * half, half), cut]
        return pltpu.make_async_copy((d0, d1)[j].at[:, cut], target, down_sem.at[n, j])

    def out_copy(n):
        cut = pl.ds(n * WIDE, WIDE)
        return pltpu.make_async_copy(outs.at[:, cut], out_ref.at[:, cut], out_sem.at[n])

    for k in range(deep_count):
        x_copy(k).start()
        for j in range(4):
            in_copy(k, j).start()
    for n in range(wide_count):
        for j in range(2):
            down_copy(n, j).start()
    for k in range(deep_count):
        x_copy(k).wait()
        for j in range(4):
            in_copy(k, j).wait()
        cut = slice(k * DEEP, (k + 1) * DEEP)
        product = dot(x[:, cut], w_in[cut, :])
        if k == 0:
            acc[...] = product
        else:
            acc[...] += product
    gate, up = acc[:, :units], acc[:, units:]
    hidden[...] = (gate / (1.0 + jnp.exp(-gate)) * up).astype(jnp.bfloat16)
    for n in range(wide_count):
        for j in range(2):
            down_copy(n, j).wait()
        cut = slice(n * WIDE, (n + 1) * WIDE)
        outs[:, cut] = dot(hidden[...], w_out[:, cut]).astype(jnp.bfloat16)
        out_copy(n).start()
    for n in range(wide_count):
        out_copy(n).wait()


def expert_rows(rows, gates, ups, downs):
    slots, width = rows.shape
    half = gates[0].shape[1]
    units = 2 * half
    deep_count, wide_count = width // DEEP, width // WIDE
    anywhere = pl.BlockSpec(memory_space=pl.ANY)
    return pl.pallas_call(
        expert_kernel,
        out_shape=jax.ShapeDtypeStruct((slots, width), jnp.bfloat16),
        in_specs=[anywhere] * 7,
        out_specs=anywhere,
        scratch_shapes=[
            pltpu.VMEM((slots, width), jnp.bfloat16),
            pltpu.VMEM((width, 2 * units), jnp.bfloat16),
            pltpu.VMEM((units, width), jnp.bfloat16),
            pltpu.VMEM((slots, 2 * units), jnp.float32),
            pltpu.VMEM((slots, units), jnp.bfloat16),
            pltpu.VMEM((slots, width), jnp.bfloat16),
            pltpu.SemaphoreType.DMA((deep_count,)),
            pltpu.SemaphoreType.DMA((deep_count, 4)),
            pltpu.SemaphoreType.DMA((wide_count, 2)),
            pltpu.SemaphoreType.DMA((wide_count,)),
        ],
        compiler_params=pltpu.CompilerParams(vmem_limit_bytes=44 * 1024 * 1024),
        cost_estimate=pl.CostEstimate(
            flops=6 * slots * width * units,
            bytes_accessed=2 * (3 * width * units + 2 * slots * width),
            transcendentals=slots * units,
        ),
    )(rows, *gates, *ups, *downs)


def route_slots(route_ids, experts, capacity):
    rows = route_ids.shape[0]
    ids = jnp.arange(experts, dtype=jnp.int32)
    named = jnp.any(route_ids[:, :, None] == ids[None, None, :], axis=1)
    earlier = jnp.arange(rows)[:, None] > jnp.arange(rows)[None, :]
    position = dot(earlier.astype(jnp.bfloat16), named.astype(jnp.bfloat16))
    position = jnp.where(named, position, -1.0).T
    slots = jnp.arange(capacity, dtype=jnp.float32)
    onehot = position[:, None, :] == slots[None, :, None]
    return named, onehot


def body(flight, norm_gain, router, w_gate, w_up, w_down, routes):
    rows = flight.shape[1]
    experts = router.shape[2]
    ticks = routes.shape[1]
    top_count = routes.shape[3]
    capacity = 2 * min(rows // 2, 3 * rows * top_count // (4 * experts))
    slot_count = experts * capacity
    gates = (w_gate[0], to_core(w_gate[0]))
    ups = (w_up[0], to_core(w_up[0]))
    downs = (w_down[0], to_core(w_down[0]))

    current = flight[0]
    for tick in range(ticks):
        named, onehot = route_slots(routes[0, tick], experts, capacity)
        pick = onehot.reshape(slot_count, rows).astype(jnp.bfloat16)
        float_state = current.astype(jnp.float32)
        normed = (
            float_state
            * lax.rsqrt(jnp.mean(float_state * float_state, axis=-1, keepdims=True) + 1e-06)
            * norm_gain[0][None, :]
        ).astype(jnp.bfloat16)
        normed = lax.optimization_barrier(normed)
        arrived = exchanged(dot(pick, normed).astype(jnp.bfloat16), experts)
        logits = dot(normed, router[0])
        raised = jnp.where(named, jnp.exp(logits), 0.0)
        mix_weight = raised / jnp.sum(raised, axis=1, keepdims=True)
        spread = jnp.where(onehot, mix_weight.T[:, None, :], 0.0).reshape(slot_count, rows).T
        spread_high, spread_low = split_high_low(spread)
        outs = expert_rows(arrived, gates, ups, downs)
        returned = exchanged(outs, experts)
        moe = dot(spread_high, returned) + dot(spread_low, returned)
        current = to_next((float_state + moe).astype(jnp.bfloat16))
    return current[None]


def solution(mesh):
    return jax.shard_map(
        body,
        mesh=mesh,
        in_specs=(
            P("pipe", "expert", None),
            P("pipe", None),
            P("pipe", None, None),
            P("pipe", None, "expert"),
            P("pipe", None, "expert"),
            P("pipe", "expert", None),
            P("pipe", None, "expert", None),
        ),
        out_specs=P("pipe", "expert", None),
        check_vma=False,
    )
```

```python
import functools

import jax
import jax.numpy as jnp
from jax import lax
from jax.experimental import pallas as pl
from jax.experimental.pallas import tpu as pltpu
from jax.sharding import PartitionSpec as P

DEEP = 1024
WIDE = 1024
GROUPS = ((0, 2, 5, 7), (4, 6, 1, 3))
CHAIN = True


def dot(a, b):
    return jnp.dot(a, b, preferred_element_type=jnp.float32)


def split_high_low(value):
    high = value.astype(jnp.bfloat16)
    return high, (value - high.astype(jnp.float32)).astype(jnp.bfloat16)


def to_core(value):
    count = lax.axis_size("expert")
    return lax.ppermute(value, "expert", [(d, d ^ 1) for d in range(count)])


def to_next(value):
    sections = lax.axis_size("pipe")
    return lax.ppermute(value, "pipe", [(p, (p + 1) % sections) for p in range(sections)])


def moved(value, flip):
    count = lax.axis_size("expert")
    if flip == 0:
        return value
    return lax.ppermute(value, "expert", [(d, d ^ (2 * flip)) for d in range(count)])


def expert_kernel(blocks, *refs):
    x_refs, (g0, g1, u0, u1, d0, d1) = refs[:blocks], refs[blocks : blocks + 6]
    out_refs = refs[blocks + 6 : 2 * blocks + 6]
    x, w_in, w_out, acc, hidden, outs, x_sem, in_sem, down_sem, out_sem = refs[2 * blocks + 6 :]
    rows, width = x_refs[0].shape
    half = g0.shape[1]
    units = 2 * half
    deep_count, wide_count = width // DEEP, width // WIDE

    def x_copy(k, b):
        cut = pl.ds(k * DEEP, DEEP)
        target = x.at[pl.ds(b * rows, rows), cut]
        return pltpu.make_async_copy(x_refs[b].at[:, cut], target, x_sem.at[k, b])

    def in_copy(k, j):
        source = (g0, g1, u0, u1)[j]
        cut = pl.ds(k * DEEP, DEEP)
        target = w_in.at[cut, pl.ds(j * half, half)]
        return pltpu.make_async_copy(source.at[cut, :], target, in_sem.at[k, j])

    def down_copy(n, j):
        cut = pl.ds(n * WIDE, WIDE)
        target = w_out.at[pl.ds(j * half, half), cut]
        return pltpu.make_async_copy((d0, d1)[j].at[:, cut], target, down_sem.at[n, j])

    def out_copy(n, b):
        cut = pl.ds(n * WIDE, WIDE)
        source = outs.at[pl.ds(b * rows, rows), cut]
        return pltpu.make_async_copy(source, out_refs[b].at[:, cut], out_sem.at[n, b])

    for k in range(deep_count):
        for b in range(blocks):
            x_copy(k, b).start()
        for j in range(4):
            in_copy(k, j).start()
    for n in range(wide_count):
        for j in range(2):
            down_copy(n, j).start()
    for k in range(deep_count):
        for b in range(blocks):
            x_copy(k, b).wait()
        for j in range(4):
            in_copy(k, j).wait()
        cut = slice(k * DEEP, (k + 1) * DEEP)
        product = dot(x[:, cut], w_in[cut, :])
        if k == 0:
            acc[...] = product
        else:
            acc[...] += product
    gate, up = acc[:, :units], acc[:, units:]
    hidden[...] = (gate / (1.0 + jnp.exp(-gate)) * up).astype(jnp.bfloat16)
    for n in range(wide_count):
        for j in range(2):
            down_copy(n, j).wait()
        cut = slice(n * WIDE, (n + 1) * WIDE)
        outs[:, cut] = dot(hidden[...], w_out[:, cut]).astype(jnp.bfloat16)
        for b in range(blocks):
            out_copy(n, b).start()
    for n in range(wide_count):
        for b in range(blocks):
            out_copy(n, b).wait()


def expert_rows(rows, gates, ups, downs):
    blocks, (height, width) = len(rows), rows[0].shape
    slots = blocks * height
    half = gates[0].shape[1]
    units = 2 * half
    deep_count, wide_count = width // DEEP, width // WIDE
    anywhere = pl.BlockSpec(memory_space=pl.ANY)
    return pl.pallas_call(
        functools.partial(expert_kernel, blocks),
        out_shape=[jax.ShapeDtypeStruct((height, width), jnp.bfloat16)] * blocks,
        in_specs=[anywhere] * (blocks + 6),
        out_specs=[anywhere] * blocks,
        scratch_shapes=[
            pltpu.VMEM((slots, width), jnp.bfloat16),
            pltpu.VMEM((width, 2 * units), jnp.bfloat16),
            pltpu.VMEM((units, width), jnp.bfloat16),
            pltpu.VMEM((slots, 2 * units), jnp.float32),
            pltpu.VMEM((slots, units), jnp.bfloat16),
            pltpu.VMEM((slots, width), jnp.bfloat16),
            pltpu.SemaphoreType.DMA((deep_count, blocks)),
            pltpu.SemaphoreType.DMA((deep_count, 4)),
            pltpu.SemaphoreType.DMA((wide_count, 2)),
            pltpu.SemaphoreType.DMA((wide_count, blocks)),
        ],
        compiler_params=pltpu.CompilerParams(vmem_limit_bytes=26 * 1024 * 1024),
        cost_estimate=pl.CostEstimate(
            flops=6 * slots * width * units,
            bytes_accessed=2 * (3 * width * units + 2 * slots * width),
            transcendentals=slots * units,
        ),
    )(*rows, *gates, *ups, *downs)


def route_slots(route_ids, ids, capacity):
    rows = route_ids.shape[0]
    named = jnp.any(route_ids[:, :, None] == ids[None, None, :], axis=1)
    earlier = jnp.arange(rows)[:, None] > jnp.arange(rows)[None, :]
    position = dot(earlier.astype(jnp.bfloat16), named.astype(jnp.bfloat16))
    position = jnp.where(named, position, -1.0).T
    slots = jnp.arange(capacity, dtype=jnp.float32)
    onehot = position[:, None, :] == slots[None, :, None]
    return named, onehot


def body(flight, norm_gain, router, w_gate, w_up, w_down, routes):
    rows = flight.shape[1]
    experts = router.shape[2]
    ticks = routes.shape[1]
    top_count = routes.shape[3]
    capacity = 2 * min(rows // 2, 3 * rows * top_count // (4 * experts))
    slot_count = experts * capacity
    gates = (w_gate[0], to_core(w_gate[0]))
    ups = (w_up[0], to_core(w_up[0]))
    downs = None

    chip = lax.axis_index("expert") // 2
    ids = chip ^ jnp.array(sum(GROUPS, ()), jnp.int32)
    picked = (ids[None, :] == jnp.arange(experts, dtype=jnp.int32)[:, None]).astype(jnp.float32)
    current = flight[0]
    for tick in range(ticks):
        named, onehot = route_slots(routes[0, tick], ids, capacity)
        pick = onehot.reshape(slot_count, rows).astype(jnp.bfloat16)
        float_state = current.astype(jnp.float32)
        normed = (
            float_state
            * lax.rsqrt(jnp.mean(float_state * float_state, axis=-1, keepdims=True) + 1e-06)
            * norm_gain[0][None, :]
        ).astype(jnp.bfloat16)
        normed = lax.optimization_barrier(normed)
        outgoing = dot(pick, normed).astype(jnp.bfloat16).reshape(experts, capacity, -1)
        returned = []
        first = 0
        held = None
        for group in GROUPS:
            leaving = [outgoing[first + k] for k in range(len(group))]
            first += len(group)
            if CHAIN and held is not None:
                leaving, held = lax.optimization_barrier((leaving, held))
            arrived = [moved(block, flip) for block, flip in zip(leaving, group)]
            held = arrived
            if downs is None:
                lent, held = lax.optimization_barrier((w_down[0], held))
                downs = (w_down[0], to_core(lent))
            outs = expert_rows(held, gates, ups, downs)
            returned += [moved(block, flip) for block, flip in zip(outs, group)]
        returned = jnp.concatenate(returned, axis=0)
        logits = jnp.sum(dot(normed, router[0])[:, :, None] * picked[None], axis=1)
        raised = jnp.where(named, jnp.exp(logits), 0.0)
        mix_weight = raised / jnp.sum(raised, axis=1, keepdims=True)
        spread = jnp.where(onehot, mix_weight.T[:, None, :], 0.0).reshape(slot_count, rows).T
        spread_high, spread_low = split_high_low(spread)
        moe = dot(spread_high, returned) + dot(spread_low, returned)
        current = to_next((float_state + moe).astype(jnp.bfloat16))
    return current[None]


def solution(mesh):
    return jax.shard_map(
        body,
        mesh=mesh,
        in_specs=(
            P("pipe", "expert", None),
            P("pipe", None),
            P("pipe", None, None),
            P("pipe", None, "expert"),
            P("pipe", None, "expert"),
            P("pipe", "expert", None),
            P("pipe", None, "expert", None),
        ),
        out_specs=P("pipe", "expert", None),
        check_vma=False,
    )
```

```python
import functools

import jax
import jax.numpy as jnp
from jax import lax
from jax.experimental import pallas as pl
from jax.experimental.pallas import tpu as pltpu
from jax.sharding import PartitionSpec as P

DEEP = 1024
WIDE = 1024
GROUPS = ((4, 6, 1, 3), (0, 2, 5, 7))
CHAIN = True


def dot(a, b):
    return jnp.dot(a, b, preferred_element_type=jnp.float32)


def split_high_low(value):
    high = value.astype(jnp.bfloat16)
    return high, (value - high.astype(jnp.float32)).astype(jnp.bfloat16)


def to_core(value):
    count = lax.axis_size("expert")
    return lax.ppermute(value, "expert", [(d, d ^ 1) for d in range(count)])


def to_next(value):
    sections = lax.axis_size("pipe")
    return lax.ppermute(value, "pipe", [(p, (p + 1) % sections) for p in range(sections)])


def moved(value, flip):
    count = lax.axis_size("expert")
    if flip == 0:
        return value
    return lax.ppermute(value, "expert", [(d, d ^ (2 * flip)) for d in range(count)])


def expert_kernel(blocks, *refs):
    x_refs, (g0, g1, u0, u1, d0, d1) = refs[:blocks], refs[blocks : blocks + 6]
    out_refs = refs[blocks + 6 : 2 * blocks + 6]
    x, w_in, w_out, acc, hidden, outs, x_sem, in_sem, down_sem, out_sem = refs[2 * blocks + 6 :]
    rows, width = x_refs[0].shape
    half = g0.shape[1]
    units = 2 * half
    deep_count, wide_count = width // DEEP, width // WIDE

    def x_copy(k, b):
        cut = pl.ds(k * DEEP, DEEP)
        target = x.at[pl.ds(b * rows, rows), cut]
        return pltpu.make_async_copy(x_refs[b].at[:, cut], target, x_sem.at[k, b])

    def in_copy(k, j):
        source = (g0, g1, u0, u1)[j]
        cut = pl.ds(k * DEEP, DEEP)
        target = w_in.at[cut, pl.ds(j * half, half)]
        return pltpu.make_async_copy(source.at[cut, :], target, in_sem.at[k, j])

    def down_copy(n, j):
        cut = pl.ds(n * WIDE, WIDE)
        target = w_out.at[pl.ds(j * half, half), cut]
        return pltpu.make_async_copy((d0, d1)[j].at[:, cut], target, down_sem.at[n, j])

    def out_copy(n, b):
        cut = pl.ds(n * WIDE, WIDE)
        source = outs.at[pl.ds(b * rows, rows), cut]
        return pltpu.make_async_copy(source, out_refs[b].at[:, cut], out_sem.at[n, b])

    for k in range(deep_count):
        for b in range(blocks):
            x_copy(k, b).start()
        for j in range(4):
            in_copy(k, j).start()
    for n in range(wide_count):
        for j in range(2):
            down_copy(n, j).start()
    for k in range(deep_count):
        for b in range(blocks):
            x_copy(k, b).wait()
        for j in range(4):
            in_copy(k, j).wait()
        cut = slice(k * DEEP, (k + 1) * DEEP)
        product = dot(x[:, cut], w_in[cut, :])
        if k == 0:
            acc[...] = product
        else:
            acc[...] += product
    gate, up = acc[:, :units], acc[:, units:]
    hidden[...] = (gate / (1.0 + jnp.exp(-gate)) * up).astype(jnp.bfloat16)
    for n in range(wide_count):
        for j in range(2):
            down_copy(n, j).wait()
        cut = slice(n * WIDE, (n + 1) * WIDE)
        outs[:, cut] = dot(hidden[...], w_out[:, cut]).astype(jnp.bfloat16)
        for b in range(blocks):
            out_copy(n, b).start()
    for n in range(wide_count):
        for b in range(blocks):
            out_copy(n, b).wait()


def expert_rows(rows, gates, ups, downs):
    blocks, (height, width) = len(rows), rows[0].shape
    slots = blocks * height
    half = gates[0].shape[1]
    units = 2 * half
    deep_count, wide_count = width // DEEP, width // WIDE
    anywhere = pl.BlockSpec(memory_space=pl.ANY)
    return pl.pallas_call(
        functools.partial(expert_kernel, blocks),
        out_shape=[jax.ShapeDtypeStruct((height, width), jnp.bfloat16)] * blocks,
        in_specs=[anywhere] * (blocks + 6),
        out_specs=[anywhere] * blocks,
        scratch_shapes=[
            pltpu.VMEM((slots, width), jnp.bfloat16),
            pltpu.VMEM((width, 2 * units), jnp.bfloat16),
            pltpu.VMEM((units, width), jnp.bfloat16),
            pltpu.VMEM((slots, 2 * units), jnp.float32),
            pltpu.VMEM((slots, units), jnp.bfloat16),
            pltpu.VMEM((slots, width), jnp.bfloat16),
            pltpu.SemaphoreType.DMA((deep_count, blocks)),
            pltpu.SemaphoreType.DMA((deep_count, 4)),
            pltpu.SemaphoreType.DMA((wide_count, 2)),
            pltpu.SemaphoreType.DMA((wide_count, blocks)),
        ],
        compiler_params=pltpu.CompilerParams(vmem_limit_bytes=26 * 1024 * 1024),
        cost_estimate=pl.CostEstimate(
            flops=6 * slots * width * units,
            bytes_accessed=2 * (3 * width * units + 2 * slots * width),
            transcendentals=slots * units,
        ),
    )(*rows, *gates, *ups, *downs)


def route_slots(route_ids, ids, capacity):
    rows = route_ids.shape[0]
    named = jnp.any(route_ids[:, :, None] == ids[None, None, :], axis=1)
    earlier = jnp.arange(rows)[:, None] > jnp.arange(rows)[None, :]
    position = dot(earlier.astype(jnp.bfloat16), named.astype(jnp.bfloat16))
    position = jnp.where(named, position, -1.0).T
    slots = jnp.arange(capacity, dtype=jnp.float32)
    onehot = position[:, None, :] == slots[None, :, None]
    return named, onehot


def body(flight, norm_gain, router, w_gate, w_up, w_down, routes):
    rows = flight.shape[1]
    experts = router.shape[2]
    ticks = routes.shape[1]
    top_count = routes.shape[3]
    capacity = 2 * min(rows // 2, 3 * rows * top_count // (4 * experts))
    slot_count = experts * capacity
    gates = (w_gate[0], to_core(w_gate[0]))
    ups = downs = None

    chip = lax.axis_index("expert") // 2
    ids = chip ^ jnp.array(sum(GROUPS, ()), jnp.int32)
    picked = (ids[None, :] == jnp.arange(experts, dtype=jnp.int32)[:, None]).astype(jnp.float32)
    current = flight[0]
    for tick in range(ticks):
        named, onehot = route_slots(routes[0, tick], ids, capacity)
        pick = onehot.reshape(slot_count, rows).astype(jnp.bfloat16)
        float_state = current.astype(jnp.float32)
        normed = (
            float_state
            * lax.rsqrt(jnp.mean(float_state * float_state, axis=-1, keepdims=True) + 1e-06)
            * norm_gain[0][None, :]
        ).astype(jnp.bfloat16)
        normed = lax.optimization_barrier(normed)
        outgoing = dot(pick, normed).astype(jnp.bfloat16).reshape(experts, capacity, -1)
        returned = []
        first = 0
        held = None
        for group in GROUPS:
            leaving = [outgoing[first + k] for k in range(len(group))]
            first += len(group)
            if CHAIN and held is not None:
                leaving, held = lax.optimization_barrier((leaving, held))
            arrived = [moved(block, flip) for block, flip in zip(leaving, group)]
            held = arrived
            if downs is None:
                lent, held = lax.optimization_barrier(((w_up[0], w_down[0]), held))
                ups, downs = (w_up[0], to_core(lent[0])), (w_down[0], to_core(lent[1]))
            outs = expert_rows(held, gates, ups, downs)
            returned += [moved(block, flip) for block, flip in zip(outs, group)]
        returned = jnp.concatenate(returned, axis=0)
        logits = jnp.sum(dot(normed, router[0])[:, :, None] * picked[None], axis=1)
        raised = jnp.where(named, jnp.exp(logits), 0.0)
        mix_weight = raised / jnp.sum(raised, axis=1, keepdims=True)
        spread = jnp.where(onehot, mix_weight.T[:, None, :], 0.0).reshape(slot_count, rows).T
        spread_high, spread_low = split_high_low(spread)
        moe = dot(spread_high, returned) + dot(spread_low, returned)
        current = to_next((float_state + moe).astype(jnp.bfloat16))
    return current[None]


def solution(mesh):
    return jax.shard_map(
        body,
        mesh=mesh,
        in_specs=(
            P("pipe", "expert", None),
            P("pipe", None),
            P("pipe", None, None),
            P("pipe", None, "expert"),
            P("pipe", None, "expert"),
            P("pipe", "expert", None),
            P("pipe", None, "expert", None),
        ),
        out_specs=P("pipe", "expert", None),
        check_vma=False,
    )
```

```python
import functools

import jax
import jax.numpy as jnp
from jax import lax
from jax.experimental import pallas as pl
from jax.experimental.pallas import tpu as pltpu
from jax.sharding import PartitionSpec as P

DEEP = 1024
WIDE = 1024
GROUPS = ((4, 6, 1, 3), (0, 2, 5, 7))
CHAIN = True


def dot(a, b):
    return jnp.dot(a, b, preferred_element_type=jnp.float32)


def split_high_low(value):
    high = value.astype(jnp.bfloat16)
    return high, (value - high.astype(jnp.float32)).astype(jnp.bfloat16)


def to_core(value):
    count = lax.axis_size("expert")
    return lax.ppermute(value, "expert", [(d, d ^ 1) for d in range(count)])


def to_next(value):
    sections = lax.axis_size("pipe")
    return lax.ppermute(value, "pipe", [(p, (p + 1) % sections) for p in range(sections)])


def moved(value, flip):
    count = lax.axis_size("expert")
    if flip == 0:
        return value
    return lax.ppermute(value, "expert", [(d, d ^ (2 * flip)) for d in range(count)])


def expert_kernel(blocks, *refs):
    x_refs, (g0, g1, u0, u1, d0, d1) = refs[:blocks], refs[blocks : blocks + 6]
    out_refs = refs[blocks + 6 : 2 * blocks + 6]
    x, w_in, w_out, acc, hidden, outs, x_sem, in_sem, down_sem, out_sem = refs[2 * blocks + 6 :]
    rows, width = x_refs[0].shape
    half = g0.shape[1]
    units = 2 * half
    deep_count, wide_count = width // DEEP, width // WIDE

    def x_copy(k, b):
        cut = pl.ds(k * DEEP, DEEP)
        target = x.at[pl.ds(b * rows, rows), cut]
        return pltpu.make_async_copy(x_refs[b].at[:, cut], target, x_sem.at[k, b])

    def in_copy(k, j):
        source = (g0, g1, u0, u1)[j]
        cut = pl.ds(k * DEEP, DEEP)
        target = w_in.at[cut, pl.ds(j * half, half)]
        return pltpu.make_async_copy(source.at[cut, :], target, in_sem.at[k, j])

    def down_copy(n, j):
        cut = pl.ds(n * WIDE, WIDE)
        target = w_out.at[pl.ds(j * half, half), cut]
        return pltpu.make_async_copy((d0, d1)[j].at[:, cut], target, down_sem.at[n, j])

    def out_copy(n, b):
        cut = pl.ds(n * WIDE, WIDE)
        source = outs.at[pl.ds(b * rows, rows), cut]
        return pltpu.make_async_copy(source, out_refs[b].at[:, cut], out_sem.at[n, b])

    for k in range(deep_count):
        for b in range(blocks):
            x_copy(k, b).start()
        for j in range(4):
            in_copy(k, j).start()
    for n in range(wide_count):
        for j in range(2):
            down_copy(n, j).start()
    for k in range(deep_count):
        for b in range(blocks):
            x_copy(k, b).wait()
        for j in range(4):
            in_copy(k, j).wait()
        cut = slice(k * DEEP, (k + 1) * DEEP)
        product = dot(x[:, cut], w_in[cut, :])
        if k == 0:
            acc[...] = product
        else:
            acc[...] += product
    gate, up = acc[:, :units], acc[:, units:]
    hidden[...] = (gate / (1.0 + jnp.exp(-gate)) * up).astype(jnp.bfloat16)
    for n in range(wide_count):
        for j in range(2):
            down_copy(n, j).wait()
        cut = slice(n * WIDE, (n + 1) * WIDE)
        outs[:, cut] = dot(hidden[...], w_out[:, cut]).astype(jnp.bfloat16)
        for b in range(blocks):
            out_copy(n, b).start()
    for n in range(wide_count):
        for b in range(blocks):
            out_copy(n, b).wait()


def expert_rows(rows, gates, ups, downs):
    blocks, (height, width) = len(rows), rows[0].shape
    slots = blocks * height
    half = gates[0].shape[1]
    units = 2 * half
    deep_count, wide_count = width // DEEP, width // WIDE
    anywhere = pl.BlockSpec(memory_space=pl.ANY)
    return pl.pallas_call(
        functools.partial(expert_kernel, blocks),
        out_shape=[jax.ShapeDtypeStruct((height, width), jnp.bfloat16)] * blocks,
        in_specs=[anywhere] * (blocks + 6),
        out_specs=[anywhere] * blocks,
        scratch_shapes=[
            pltpu.VMEM((slots, width), jnp.bfloat16),
            pltpu.VMEM((width, 2 * units), jnp.bfloat16),
            pltpu.VMEM((units, width), jnp.bfloat16),
            pltpu.VMEM((slots, 2 * units), jnp.float32),
            pltpu.VMEM((slots, units), jnp.bfloat16),
            pltpu.VMEM((slots, width), jnp.bfloat16),
            pltpu.SemaphoreType.DMA((deep_count, blocks)),
            pltpu.SemaphoreType.DMA((deep_count, 4)),
            pltpu.SemaphoreType.DMA((wide_count, 2)),
            pltpu.SemaphoreType.DMA((wide_count, blocks)),
        ],
        compiler_params=pltpu.CompilerParams(vmem_limit_bytes=26 * 1024 * 1024),
        cost_estimate=pl.CostEstimate(
            flops=6 * slots * width * units,
            bytes_accessed=2 * (3 * width * units + 2 * slots * width),
            transcendentals=slots * units,
        ),
    )(*rows, *gates, *ups, *downs)


def route_slots(route_ids, chip, capacity):
    rows = route_ids.shape[0]
    flips = jnp.array(sum(GROUPS, ()), jnp.int32)
    named = jnp.any((route_ids ^ chip)[:, :, None] == flips[None, None, :], axis=1)
    earlier = jnp.arange(rows)[:, None] > jnp.arange(rows)[None, :]
    position = dot(earlier.astype(jnp.bfloat16), named.astype(jnp.bfloat16))
    position = jnp.where(named, position, -1.0).T
    slots = jnp.arange(capacity, dtype=jnp.float32)
    onehot = position[:, None, :] == slots[None, :, None]
    return named, onehot


def body(flight, norm_gain, router, w_gate, w_up, w_down, routes):
    rows = flight.shape[1]
    experts = router.shape[2]
    ticks = routes.shape[1]
    top_count = routes.shape[3]
    capacity = 2 * min(rows // 2, 3 * rows * top_count // (4 * experts))
    slot_count = experts * capacity
    gates = (w_gate[0], to_core(w_gate[0]))
    ups = downs = None

    chip = lax.axis_index("expert") // 2
    ids = chip ^ jnp.array(sum(GROUPS, ()), jnp.int32)
    picked = (ids[None, :] == jnp.arange(experts, dtype=jnp.int32)[:, None]).astype(jnp.float32)
    current = flight[0]
    for tick in range(ticks):
        named, onehot = route_slots(routes[0, tick], chip, capacity)
        pick = onehot.reshape(slot_count, rows).astype(jnp.bfloat16)
        float_state = current.astype(jnp.float32)
        normed = (
            float_state
            * lax.rsqrt(jnp.mean(float_state * float_state, axis=-1, keepdims=True) + 1e-06)
            * norm_gain[0][None, :]
        ).astype(jnp.bfloat16)
        normed = lax.optimization_barrier(normed)
        outgoing = dot(pick, normed).astype(jnp.bfloat16).reshape(experts, capacity, -1)
        returned = []
        first = 0
        held = None
        for group in GROUPS:
            leaving = [outgoing[first + k] for k in range(len(group))]
            first += len(group)
            if CHAIN and held is not None:
                leaving, held = lax.optimization_barrier((leaving, held))
            arrived = [moved(block, flip) for block, flip in zip(leaving, group)]
            held = arrived
            if downs is None:
                lent, held = lax.optimization_barrier(((w_up[0], w_down[0]), held))
                ups, downs = (w_up[0], to_core(lent[0])), (w_down[0], to_core(lent[1]))
            outs = expert_rows(held, gates, ups, downs)
            returned += [moved(block, flip) for block, flip in zip(outs, group)]
        returned = jnp.concatenate(returned, axis=0)
        logits = jnp.sum(dot(normed, router[0])[:, :, None] * picked[None], axis=1)
        raised = jnp.where(named, jnp.exp(logits), 0.0)
        mix_weight = raised / jnp.sum(raised, axis=1, keepdims=True)
        spread = jnp.where(onehot, mix_weight.T[:, None, :], 0.0).reshape(slot_count, rows).T
        spread_high, spread_low = split_high_low(spread)
        moe = dot(spread_high, returned) + dot(spread_low, returned)
        current = to_next((float_state + moe).astype(jnp.bfloat16))
    return current[None]


def solution(mesh):
    return jax.shard_map(
        body,
        mesh=mesh,
        in_specs=(
            P("pipe", "expert", None),
            P("pipe", None),
            P("pipe", None, None),
            P("pipe", None, "expert"),
            P("pipe", None, "expert"),
            P("pipe", "expert", None),
            P("pipe", None, "expert", None),
        ),
        out_specs=P("pipe", "expert", None),
        check_vma=False,
    )
```
